32 devices in a mesh: group: 2 (over y), ens: 4 (over z), row: 2 (over x), col: 2 (over core).
Axes of the slice: x: 2, y: 2, z: 4, core: 2. Of those that a mesh axis runs over, the one named last changes fastest.
Arguments:
- fields: bfloat16 [4, 128, 256, 128], P('ens', ('group', 'row'), 'col'), parts along dimension 1, may hold values from -6 to 6
- conv_weight: bfloat16 [7, 7, 128], replicated, may hold values from -0.875 to 0.875
- conv_gain: bfloat16 [128], replicated, may hold values from 0.099609375 to 1.8984375
- mlp_in: bfloat16 [128, 512], replicated, may hold values from -0.5 to 0.5
- mlp_out: bfloat16 [512, 128], replicated, may hold values from -0.25 to 0.25
- layer_scale: bfloat16 [128], replicated, may hold values from 0.099609375 to 1.8984375
- attn_gain: bfloat16 [128], replicated, may hold values from 0.099609375 to 1.8984375
- qkv_weight: bfloat16 [3, 128, 128], replicated, may hold values from -1 to 1
- out_weight: bfloat16 [128, 128], replicated, may hold values from -0.5 to 0.5
Outputs:
- result: bfloat16 [4, 128, 256, 128], P('ens', ('group', 'row'), 'col'), parts along dimension 1
The draws below stay inside these ranges and needn't reach their ends.
There are 2 independent parts, one for each index of `group`. The reference program is written for one: setup_inputs(seed, part) draws one part's arguments, and reference() takes and returns one part's arrays. A program takes and returns all parts, laid end to end along the dimension named above; an argument that names none is the same for every part. Nothing has to cross between parts.
All inputs are finite; a program needn't handle non-finite values.
Results may differ from the reference program's by a relative error of at most 0.0065.
Values may be sent and summed in bfloat16 or wider, within the bound.
A program may use at most 64 MiB of HBM per device.

```python
import math
import jax
import jax.numpy as jnp
from jax import lax

WIDTH = 128
MLP_UNITS = 512
HEADS = 4
KERNEL = 7
MEMBERS = 4
ROWS = 64
COLS = 256


def draw_qkv_weight(key, part):
    keys = jax.random.split(key, 3)
    query_part = jnp.clip(jax.random.normal(keys[0], (WIDTH, WIDTH), jnp.float32), -3.0, 3.0) / math.sqrt(WIDTH)
    key_part = jnp.clip(jax.random.normal(keys[1], (WIDTH, WIDTH), jnp.float32), -3.0, 3.0) / math.sqrt(WIDTH)
    value_part = jnp.clip(jax.random.normal(keys[2], (WIDTH, WIDTH), jnp.float32), -3.0, 3.0) / math.sqrt(WIDTH)
    return jnp.stack([query_part, key_part, value_part]).astype(jnp.bfloat16)


def block_scale(key, extent, cuts, smallest, top_value):
    gain = 1.0
    for axis_at, shards_of in cuts:
        steps = jax.random.uniform(jax.random.fold_in(jax.random.fold_in(key, 6), axis_at), (shards_of,), jnp.float32, smallest / len(cuts), top_value / len(cuts))
        gain = gain * jnp.repeat(jnp.exp(steps), extent[axis_at] // shards_of).reshape((-1,) + (1,) * (len(extent) - 1 - axis_at))
    return gain


def noise(stream_key, extent, scale, reach, cuts=(), held_as=jnp.bfloat16):
    entries = jax.random.normal(stream_key, extent, jnp.float32) * scale
    if len(cuts) > 0:
        entries = block_scale(stream_key, extent, cuts, -0.22, 0.18) * entries
    return jnp.clip(entries, min=-reach, max=reach).astype(held_as)


def setup_inputs(seed: int = 0, part: int = 0) -> dict:
    key_of = jax.random.split(jax.random.key(seed), 10)
    own_keys = jax.random.split(jax.random.fold_in(key_of[9], part), 10)
    fields = noise(own_keys[0], (MEMBERS, ROWS, COLS, WIDTH), 1.0, 6.0, ((0, 4), (1, 2), (2, 2)))
    conv_weight = noise(key_of[1], (KERNEL, KERNEL, WIDTH), (KERNEL * KERNEL) ** -0.5, 0.875)
    conv_gain = jnp.clip(1.0 + 0.18 * jax.random.normal(key_of[2], (WIDTH,), jnp.float32), 0.099609375, 1.8984375).astype(jnp.bfloat16)
    mlp_in = noise(key_of[3], (WIDTH, MLP_UNITS), WIDTH ** -0.5, 0.5)
    mlp_out = noise(key_of[4], (MLP_UNITS, WIDTH), MLP_UNITS ** -0.5, 0.25)
    layer_scale = jnp.clip(1.0 + 0.18 * jax.random.normal(key_of[5], (WIDTH,), jnp.float32), 0.099609375, 1.8984375).astype(jnp.bfloat16)
    attn_gain = jnp.clip(1.0 + 0.18 * jax.random.normal(key_of[6], (WIDTH,), jnp.float32), 0.099609375, 1.8984375).astype(jnp.bfloat16)
    qkv_weight = draw_qkv_weight(jax.random.fold_in(key_of[9], 71), part)
    out_weight = noise(key_of[8], (WIDTH, WIDTH), WIDTH ** -0.5, 0.5)
    return dict(fields=fields, conv_weight=conv_weight, conv_gain=conv_gain, mlp_in=mlp_in, mlp_out=mlp_out, layer_scale=layer_scale, attn_gain=attn_gain, qkv_weight=qkv_weight, out_weight=out_weight)


def layer_norm(values, gain_vec):
    center = values - lax.optimization_barrier(jnp.mean(values, axis=-1, keepdims=True))
    spread = lax.optimization_barrier(jnp.mean(center * center, axis=-1, keepdims=True))
    return center * lax.rsqrt(spread + 1e-06) * gain_vec.astype(jnp.float32)

def mix_members(flat_rows, attn_gain, qkv_weight):
    count, pixels, width = flat_rows.shape
    head_dim = width // HEADS
    normed = layer_norm(flat_rows.astype(jnp.float32), attn_gain).astype(jnp.bfloat16)
    project = jnp.einsum('mpc,jcd->jmpd', normed.astype(jnp.float32), qkv_weight.astype(jnp.float32)).astype(jnp.bfloat16)
    split = project.reshape(3, count, pixels, HEADS, head_dim)
    scores = jnp.einsum('mphd,nphd->hmnp', split[0].astype(jnp.float32), split[1].astype(jnp.float32)) * head_dim ** (-0.5)
    top = lax.optimization_barrier(jnp.max(scores, axis=2, keepdims=True))
    expo = jnp.exp(scores - top)
    weights = (expo / lax.optimization_barrier(jnp.sum(expo, axis=2, keepdims=True))).astype(jnp.bfloat16)
    mixed = jnp.einsum('hmnp,nphd->mphd', weights.astype(jnp.float32), split[2].astype(jnp.float32)).astype(jnp.bfloat16)
    return mixed.reshape(count, pixels, width)

def reference(fields, conv_weight, conv_gain, mlp_in, mlp_out, layer_scale, attn_gain, qkv_weight, out_weight):

    def convnext(member):
        rows, cols, width = member.shape
        padded = jnp.pad(member, ((3, 3), (3, 3), (0, 0)))
        total = jnp.zeros((rows, cols, width), jnp.float32)
        for row_tap in range(KERNEL):
            for col_tap in range(KERNEL):
                total = total + padded[row_tap:row_tap + rows, col_tap:col_tap + cols, :].astype(jnp.float32) * conv_weight[row_tap, col_tap].astype(jnp.float32)
        normed = layer_norm(total, conv_gain).astype(jnp.bfloat16).reshape(rows * cols, width)
        inner = jax.nn.gelu(jnp.dot(normed, mlp_in, preferred_element_type=jnp.float32), approximate=True).astype(jnp.bfloat16)
        branch = jnp.dot(inner, mlp_out, preferred_element_type=jnp.float32).reshape(rows, cols, width)
        return (member.astype(jnp.float32) + layer_scale.astype(jnp.float32) * branch).astype(jnp.bfloat16)
    middle = lax.map(convnext, fields)

    def per_row(block):
        mixed = mix_members(block, attn_gain, qkv_weight)
        count, pixels, width = mixed.shape
        projected = jnp.dot(mixed.reshape(count * pixels, width), out_weight, preferred_element_type=jnp.float32).reshape(count, pixels, width)
        return (block.astype(jnp.float32) + projected).astype(jnp.bfloat16)
    rows_first = jnp.swapaxes(middle, 0, 1)
    done = lax.map(per_row, rows_first)
    return jnp.swapaxes(done, 0, 1)
```

```python
import functools
import math

import jax
import jax.numpy as jnp
from jax import lax
from jax.experimental import pallas as pl
from jax.experimental.pallas import tpu as pltpu
from jax.sharding import PartitionSpec as P

HEADS = 4
KERNEL = 7
HALO = KERNEL // 2
PAD = 16
MESH = pl.DeviceIdType.MESH
F32 = jnp.float32
BF16 = jnp.bfloat16
SIDES = [(a, b) for a in (-1, 0, 1) for b in (-1, 0, 1) if (a, b) != (0, 0)]


def norm(values, gain):
    center = values - jnp.mean(values, axis=-1, keepdims=True)
    spread = jnp.mean(center * center, axis=-1, keepdims=True)
    return (center * lax.rsqrt(spread + 1e-06) * gain).astype(BF16)


def gelu(h):
    inner = h * (0.7978845608028654 + 0.035677408136300125 * (h * h))
    return (0.5 * h) * (1.0 + jnp.tanh(inner))


def kernel(
    n, row_n, col_n, sub,
    fields, conv_weight, conv_gain, mlp_in, mlp_out, layer_scale, attn_gain, qkv, out_weight,
    out,
    pad, taps, conv, mid, recv, back, q_s, k_s, v_s, halo_rows, halo_cols, halo_corner,
    halo_send, halo_recv, send1, recv1, send2, recv2,
):
    _, rows, cols, width = fields.shape
    share = rows // n
    steps = share // sub
    me = lax.axis_index("ens")
    row_i = lax.axis_index("row")
    col_i = lax.axis_index("col")
    barrier = pltpu.get_barrier_semaphore()

    def exists(a, b):
        ok = None
        for d, i, size in ((a, row_i, row_n), (b, col_i, col_n)):
            if d == 0:
                continue
            one = i > 0 if d < 0 else i < size - 1
            ok = one if ok is None else jnp.logical_and(ok, one)
        return ok

    def other(k):
        return lax.rem(me + 1 + k, n)

    for a, b in SIDES:
        @pl.when(exists(a, b))
        def _(a=a, b=b):
            pl.semaphore_signal(
                barrier, inc=1, device_id={"row": row_i + a, "col": col_i + b}, device_id_type=MESH
            )

    @pl.loop(0, n - 1)
    def _(k):
        pl.semaphore_signal(barrier, inc=1, device_id={"ens": other(k)}, device_id_type=MESH)

    def around(i, size):
        return jnp.where(i > 0, 1, 0) + jnp.where(i < size - 1, 1, 0) + 1

    pl.semaphore_wait(barrier, around(row_i, row_n) * around(col_i, col_n) + (n - 2))

    def halo_ref(a, b):
        if b == 0:
            return halo_rows.at[0 if a < 0 else 1]
        if a == 0:
            return halo_cols.at[0 if b < 0 else 1]
        return halo_corner.at[(0 if a < 0 else 2) + (0 if b < 0 else 1)]

    def halo_copy(a, b):
        r = slice(0, rows) if a == 0 else (slice(0, HALO) if a < 0 else slice(rows - HALO, rows))
        c = slice(0, cols) if b == 0 else (slice(0, PAD) if b < 0 else slice(cols - PAD, cols))
        return pltpu.make_async_remote_copy(
            src_ref=fields.at[0, r, c, :],
            dst_ref=halo_ref(-a, -b),
            send_sem=halo_send.at[SIDES.index((a, b))],
            recv_sem=halo_recv.at[SIDES.index((-a, -b))],
            device_id={"row": row_i + a, "col": col_i + b},
            device_id_type=MESH,
        )

    for a, b in SIDES:
        @pl.when(exists(a, b))
        def _(a=a, b=b):
            halo_copy(a, b).start()

    for a in range(KERNEL):
        taps[a, 0:KERNEL, :] = conv_weight[a].astype(F32)

    @pl.loop(0, rows)
    def _(r):
        pad[HALO + r, PAD : PAD + cols, :] = fields[0, r].astype(F32)

    def spot(a, b):
        r = slice(HALO, HALO + rows) if a == 0 else (
            slice(0, HALO) if a < 0 else slice(HALO + rows, 2 * HALO + rows))
        c = slice(PAD, PAD + cols) if b == 0 else (
            slice(0, PAD) if b < 0 else slice(PAD + cols, 2 * PAD + cols))
        return r, c

    for a, b in SIDES:
        here = exists(a, b)
        r, c = spot(a, b)

        @pl.when(here)
        def _(a=a, b=b, r=r, c=c):
            pltpu.make_async_remote_copy(
                src_ref=halo_ref(a, b),
                dst_ref=halo_ref(a, b),
                send_sem=halo_send.at[SIDES.index((a, b))],
                recv_sem=halo_recv.at[SIDES.index((a, b))],
                device_id={"row": row_i + a, "col": col_i + b},
                device_id_type=MESH,
            ).wait_recv()
            pad[r, c, :] = halo_ref(a, b)[...].astype(F32)

        @pl.when(jnp.logical_not(here))
        def _(r=r, c=c):
            pad[r, c, :] = jnp.zeros((r.stop - r.start, c.stop - c.start, width), F32)

    gain1 = conv_gain[...].astype(F32).reshape(1, width)
    gain2 = attn_gain[...].astype(F32).reshape(1, width)
    scale = layer_scale[...].astype(F32).reshape(1, width)
    head = width // HEADS
    ones = (
        lax.broadcasted_iota(jnp.int32, (width, width), 0) // head
        == lax.broadcasted_iota(jnp.int32, (width, width), 1) // head
    ).astype(F32).astype(BF16)
    factor = head**-0.5 * math.log2(math.e)

    def to_mixer(s, d):
        return pltpu.make_async_remote_copy(
            src_ref=mid.at[s, d],
            dst_ref=recv.at[s, me],
            send_sem=send1.at[s, d],
            recv_sem=recv1.at[s, me],
            device_id={"ens": d},
            device_id_type=MESH,
        )

    def from_member(s, d):
        return pltpu.make_async_remote_copy(
            src_ref=mid.at[s, d],
            dst_ref=recv.at[s, d],
            send_sem=send1.at[s, d],
            recv_sem=recv1.at[s, d],
            device_id={"ens": d},
            device_id_type=MESH,
        )

    def to_member(s, d):
        return pltpu.make_async_remote_copy(
            src_ref=back.at[s, d],
            dst_ref=out.at[0, pl.ds(me * share + s * sub, sub)],
            send_sem=send2.at[s, d],
            recv_sem=recv2.at[s, me],
            device_id={"ens": d},
            device_id_type=MESH,
        )

    def from_mixer(s, d):
        return pltpu.make_async_remote_copy(
            src_ref=back.at[s, d],
            dst_ref=out.at[0, pl.ds(d * share + s * sub, sub)],
            send_sem=send2.at[s, d],
            recv_sem=recv2.at[s, d],
            device_id={"ens": d},
            device_id_type=MESH,
        )

    def block(s, k):
        d = other(k)
        first = d * share + s * sub

        @pl.loop(0, cols // 16)
        def _(j):
            c0 = j * 16
            acc = [jnp.zeros((16, width), F32) for _ in range(sub)]
            for b in range(KERNEL):
                lines = [
                    pad[first + r, pl.ds(c0 + (PAD - HALO + b), 16), :]
                    for r in range(sub + KERNEL - 1)
                ]
                for a in range(KERNEL):
                    w = taps[a, b : b + 1, :]
                    acc = [acc[r] + lines[r + a] * w for r in range(sub)]
            for r in range(sub):
                conv[r, pl.ds(pl.multiple_of(c0, 16), 16), :] = acc[r]

        for r in range(sub):
            normed = norm(conv[r], gain1)
            h = jnp.dot(normed, mlp_in[...], preferred_element_type=F32)
            inner = gelu(h).astype(BF16)
            branch = jnp.dot(inner, mlp_out[...], preferred_element_type=F32)
            mid[s, d, r] = (fields[0, first + r].astype(F32) + scale * branch).astype(BF16)

        @pl.when(k < n - 1)
        def _():
            to_mixer(s, d).start()

        @pl.when(k == n - 1)
        def _():
            recv[s, me] = mid[s, me]

    few = n <= 8

    def each_member(body):
        if few:
            for m in range(n):
                body(m)
        else:
            pl.loop(0, n)(body)

    def mix(s):
        @pl.loop(0, n - 1)
        def _(k):
            from_member(s, other(k)).wait_recv()

        @pl.loop(0, sub)
        def _(r):
            def project(m):
                normed = norm(recv[s, m, r].astype(F32), gain2)
                q_s[m] = jnp.dot(normed, qkv[0], preferred_element_type=F32).astype(BF16)
                k_s[m] = jnp.dot(normed, qkv[1], preferred_element_type=F32).astype(BF16)
                v_s[m] = jnp.dot(normed, qkv[2], preferred_element_type=F32).astype(BF16)

            def attend(m):
                def score(j):
                    prod = q_s[m].astype(F32) * k_s[j].astype(F32)
                    return jnp.dot(prod.astype(BF16), ones, preferred_element_type=F32)

                if few:
                    scores = [score(j) for j in range(n)]
                    top = functools.reduce(jnp.maximum, scores)
                    den, acc = None, None
                    for j in range(n):
                        e = jnp.exp2((scores[j] - top) * factor)
                        term = e * v_s[j].astype(F32)
                        den = e if den is None else den + e
                        acc = term if acc is None else acc + term
                else:
                    def more(j, carry):
                        top, den, acc = carry
                        sc = score(j)
                        now = jnp.maximum(top, sc)
                        keep = jnp.exp2((top - now) * factor)
                        e = jnp.exp2((sc - now) * factor)
                        return now, den * keep + e, acc * keep + e * v_s[j].astype(F32)

                    _, den, acc = lax.fori_loop(
                        1, n, more,
                        (score(0), jnp.ones((cols, width), F32), v_s[0].astype(F32)),
                    )
                mixed = (acc / den).astype(BF16)
                proj = jnp.dot(mixed, out_weight[...], preferred_element_type=F32)
                back[s, m, r] = (recv[s, m, r].astype(F32) + proj).astype(BF16)

            each_member(project)
            each_member(attend)

        @pl.loop(0, n - 1)
        def _(k):
            to_member(s, other(k)).start()

        out[0, pl.ds(me * share + s * sub, sub)] = back[s, me]

    @pl.loop(0, steps + 1)
    def _(s):
        @pl.when(s < steps)
        def _():
            pl.loop(0, n)(lambda k: block(s, k))

        @pl.when(s >= 1)
        def _():
            mix(s - 1)

    for a, b in SIDES:
        @pl.when(exists(a, b))
        def _(a=a, b=b):
            halo_copy(a, b).wait_send()

    @pl.loop(0, steps)
    def _(s):
        @pl.loop(0, n - 1)
        def _(k):
            d = other(k)
            to_mixer(s, d).wait_send()
            to_member(s, d).wait_send()
            from_mixer(s, d).wait_recv()


SUB = 4


def shards(n, row_n, col_n, *args):
    fields = args[0]
    _, rows, cols, width = fields.shape
    share = rows // n
    sub = math.gcd(share, SUB)
    steps = share // sub
    vmem = pl.BlockSpec(memory_space=pltpu.VMEM)
    dma = pltpu.SemaphoreType.DMA
    blocks = (steps, n, sub, cols, width)
    return pl.pallas_call(
        functools.partial(kernel, n, row_n, col_n, sub),
        out_shape=jax.ShapeDtypeStruct(fields.shape, fields.dtype),
        in_specs=[vmem] * len(args),
        out_specs=vmem,
        scratch_shapes=[
            pltpu.VMEM((rows + 2 * HALO, cols + 2 * PAD, width), F32),
            pltpu.VMEM((KERNEL, 8, width), F32),
            pltpu.VMEM((sub, cols, width), F32),
            pltpu.VMEM(blocks, BF16),
            pltpu.VMEM(blocks, BF16),
            pltpu.VMEM(blocks, BF16),
            pltpu.VMEM((n, cols, width), BF16),
            pltpu.VMEM((n, cols, width), BF16),
            pltpu.VMEM((n, cols, width), BF16),
            pltpu.VMEM((2, HALO, cols, width), BF16),
            pltpu.VMEM((2, rows, PAD, width), BF16),
            pltpu.VMEM((4, HALO, PAD, width), BF16),
            dma((8,)),
            dma((8,)),
            dma((steps, n)),
            dma((steps, n)),
            dma((steps, n)),
            dma((steps, n)),
        ],
        compiler_params=pltpu.CompilerParams(
            collective_id=0, has_side_effects=True, vmem_limit_bytes=48 * 1024 * 1024
        ),
    )(*args)


def solution(mesh):
    size = mesh.shape
    return jax.shard_map(
        functools.partial(shards, size["ens"], size["row"], size["col"]),
        mesh=mesh,
        in_specs=(P("ens", ("group", "row"), "col", None), P(), P(), P(), P(), P(), P(), P(), P()),
        out_specs=P("ens", ("group", "row"), "col", None),
        check_vma=False,
    )
```

```python
import functools
import math

import jax
import jax.numpy as jnp
from jax import lax
from jax.experimental import pallas as pl
from jax.experimental.pallas import tpu as pltpu
from jax.sharding import PartitionSpec as P

HEADS = 4
KERNEL = 7
HALO = KERNEL // 2
PAD = 16
MESH = pl.DeviceIdType.MESH
F32 = jnp.float32
BF16 = jnp.bfloat16
SIDES = [(a, b) for a in (-1, 0, 1) for b in (-1, 0, 1) if (a, b) != (0, 0)]


def norm(values, gain):
    center = values - jnp.mean(values, axis=-1, keepdims=True)
    spread = jnp.mean(center * center, axis=-1, keepdims=True)
    return (center * lax.rsqrt(spread + 1e-06) * gain).astype(BF16)


def gelu(h):
    inner = h * (0.7978845608028654 + 0.035677408136300125 * (h * h))
    return (0.5 * h) * (1.0 + jnp.tanh(inner))


def kernel(
    n, row_n, col_n, sub,
    fields_hbm, *refs,
):
    count = 8
    weights_hbm, out, weights = refs[:count], refs[count], refs[count + 1 : 2 * count + 1]
    fields, load = refs[2 * count + 1 : 2 * count + 3]
    conv_weight, conv_gain, mlp_in, mlp_out, layer_scale, attn_gain, qkv, out_weight = weights
    (
    pad, taps, conv, mid, recv, back, q_s, k_s, v_s, qkv_s, halo_rows, halo_cols, halo_corner,
    halo_send, halo_recv, send1, recv1, send2, recv2,
    ) = refs[2 * count + 3 :]
    _, rows, cols, width = fields.shape
    share = rows // n
    steps = share // sub
    me = lax.axis_index("ens")
    row_i = lax.axis_index("row")
    col_i = lax.axis_index("col")
    loads = [
        pltpu.make_async_copy(src, dst, load.at[i])
        for i, (src, dst) in enumerate(zip((fields_hbm, *weights_hbm), (fields, *weights)))
    ]
    for copy in loads:
        copy.start()
    barrier = pltpu.get_barrier_semaphore()

    def exists(a, b):
        ok = None
        for d, i, size in ((a, row_i, row_n), (b, col_i, col_n)):
            if d == 0:
                continue
            one = i > 0 if d < 0 else i < size - 1
            ok = one if ok is None else jnp.logical_and(ok, one)
        return ok

    half = n // 2 if n % 2 == 0 else n

    def other(k):
        if n % 2:
            return lax.rem(me + 1 + k, n)
        side = me // half
        far = (1 - side) * half + lax.rem(me + k, half)
        near = side * half + lax.rem(me + 1 + k, half)
        return jnp.where(k < half, far, near)

    for a, b in SIDES:
        @pl.when(exists(a, b))
        def _(a=a, b=b):
            pl.semaphore_signal(
                barrier, inc=1, device_id={"row": row_i + a, "col": col_i + b}, device_id_type=MESH
            )

    @pl.loop(0, n - 1)
    def _(k):
        pl.semaphore_signal(barrier, inc=1, device_id={"ens": other(k)}, device_id_type=MESH)

    def around(i, size):
        return jnp.where(i > 0, 1, 0) + jnp.where(i < size - 1, 1, 0) + 1

    pl.semaphore_wait(barrier, around(row_i, row_n) * around(col_i, col_n) + (n - 2))

    def halo_ref(a, b):
        if b == 0:
            return halo_rows.at[0 if a < 0 else 1]
        if a == 0:
            return halo_cols.at[0 if b < 0 else 1]
        return halo_corner.at[(0 if a < 0 else 2) + (0 if b < 0 else 1)]

    def halo_copy(a, b):
        r = slice(0, rows) if a == 0 else (slice(0, HALO) if a < 0 else slice(rows - HALO, rows))
        c = slice(0, cols) if b == 0 else (slice(0, PAD) if b < 0 else slice(cols - PAD, cols))
        return pltpu.make_async_remote_copy(
            src_ref=fields_hbm.at[0, r, c, :],
            dst_ref=halo_ref(-a, -b),
            send_sem=halo_send.at[SIDES.index((a, b))],
            recv_sem=halo_recv.at[SIDES.index((-a, -b))],
            device_id={"row": row_i + a, "col": col_i + b},
            device_id_type=MESH,
        )

    for a, b in SIDES:
        @pl.when(exists(a, b))
        def _(a=a, b=b):
            halo_copy(a, b).start()

    for copy in loads:
        copy.wait()
    for j in range(3):
        qkv_s[:, j * width : (j + 1) * width] = qkv[j]
    for a in range(KERNEL):
        taps[a, 0:KERNEL, :] = conv_weight[a].astype(F32)

    @pl.loop(0, rows)
    def _(r):
        pad[HALO + r, PAD : PAD + cols, :] = fields[0, r].astype(F32)

    def spot(a, b):
        r = slice(HALO, HALO + rows) if a == 0 else (
            slice(0, HALO) if a < 0 else slice(HALO + rows, 2 * HALO + rows))
        c = slice(PAD, PAD + cols) if b == 0 else (
            slice(0, PAD) if b < 0 else slice(PAD + cols, 2 * PAD + cols))
        return r, c

    for a, b in SIDES:
        here = exists(a, b)
        r, c = spot(a, b)

        @pl.when(here)
        def _(a=a, b=b, r=r, c=c):
            pltpu.make_async_remote_copy(
                src_ref=halo_ref(a, b),
                dst_ref=halo_ref(a, b),
                send_sem=halo_send.at[SIDES.index((a, b))],
                recv_sem=halo_recv.at[SIDES.index((a, b))],
                device_id={"row": row_i + a, "col": col_i + b},
                device_id_type=MESH,
            ).wait_recv()
            pad[r, c, :] = halo_ref(a, b)[...].astype(F32)

        @pl.when(jnp.logical_not(here))
        def _(r=r, c=c):
            pad[r, c, :] = jnp.zeros((r.stop - r.start, c.stop - c.start, width), F32)

    gain1 = conv_gain[...].astype(F32).reshape(1, width)
    gain2 = attn_gain[...].astype(F32).reshape(1, width)
    scale = layer_scale[...].astype(F32).reshape(1, width)
    head = width // HEADS
    ones = (
        lax.broadcasted_iota(jnp.int32, (2 * width, 2 * width), 0) // head
        == lax.broadcasted_iota(jnp.int32, (2 * width, 2 * width), 1) // head
    ).astype(F32).astype(BF16)
    factor = head**-0.5 * math.log2(math.e)

    def to_mixer(s, d, r):
        return pltpu.make_async_remote_copy(
            src_ref=mid.at[s, d, r],
            dst_ref=recv.at[s, me, r],
            send_sem=send1.at[s, d, r],
            recv_sem=recv1.at[s, me, r],
            device_id={"ens": d},
            device_id_type=MESH,
        )

    def from_member(s, d, r):
        return pltpu.make_async_remote_copy(
            src_ref=mid.at[s, d, r],
            dst_ref=recv.at[s, d, r],
            send_sem=send1.at[s, d, r],
            recv_sem=recv1.at[s, d, r],
            device_id={"ens": d},
            device_id_type=MESH,
        )

    def to_member(s, d, r):
        return pltpu.make_async_remote_copy(
            src_ref=back.at[s, d, r],
            dst_ref=out.at[0, me * share + s * sub + r],
            send_sem=send2.at[s, d, r],
            recv_sem=recv2.at[s, me, r],
            device_id={"ens": d},
            device_id_type=MESH,
        )

    def from_mixer(s, d, r):
        return pltpu.make_async_remote_copy(
            src_ref=back.at[s, d, r],
            dst_ref=out.at[0, d * share + s * sub + r],
            send_sem=send2.at[s, d, r],
            recv_sem=recv2.at[s, d, r],
            device_id={"ens": d},
            device_id_type=MESH,
        )

    def block(s, k):
        d = other(k)
        first = d * share + s * sub

        @pl.loop(0, cols // 16)
        def _(j):
            c0 = j * 16
            acc = [jnp.zeros((16, width), F32) for _ in range(sub)]
            for b in range(KERNEL):
                lines = [
                    pad[first + r, pl.ds(c0 + (PAD - HALO + b), 16), :]
                    for r in range(sub + KERNEL - 1)
                ]
                for a in range(KERNEL):
                    w = taps[a, b : b + 1, :]
                    acc = [acc[r] + lines[r + a] * w for r in range(sub)]
            for r in range(sub):
                conv[r, pl.ds(pl.multiple_of(c0, 16), 16), :] = acc[r]

        normed = norm(conv[...].reshape(sub * cols, width), gain1)
        branch = jnp.zeros((sub * cols, width), F32)
        units = mlp_in.shape[1]
        for u in range(0, units, units // 2):
            part = slice(u, u + units // 2)
            h = jnp.dot(normed, mlp_in[:, part], preferred_element_type=F32)
            inner = gelu(h).astype(BF16)
            branch = branch + jnp.dot(inner, mlp_out[part, :], preferred_element_type=F32)
        branch = (scale * branch).reshape(sub, cols, width)
        for r in range(sub):
            mid[s, d, r] = (fields[0, first + r].astype(F32) + branch[r]).astype(BF16)

            @pl.when(k < n - 1)
            def _(r=r):
                to_mixer(s, d, r).start()

        @pl.when(k == n - 1)
        def _():
            recv[s, me] = mid[s, me]

    few = n <= 8

    def mix(s):
        @pl.loop(0, sub)
        def _(r):
            @pl.loop(0, n - 1)
            def _(k):
                from_member(s, other(k), r).wait_recv()

            def project(m, many):
                x = recv[s, pl.ds(m, many), r].astype(F32).reshape(many * cols, width)
                normed = norm(x, gain2)
                got = jnp.dot(normed, qkv_s[...], preferred_element_type=F32)
                got = got.reshape(many, cols, 3 * width)
                q_s[pl.ds(m, many)] = got[:, :, 0:width].astype(BF16)
                k_s[pl.ds(m, many)] = got[:, :, width : 2 * width].astype(BF16)
                v_s[pl.ds(m, many)] = got[:, :, 2 * width :].astype(BF16).astype(F32)

            def attend(k):
                m = other(k)
                query = q_s[m]

                def score(*js):
                    prod = jnp.concatenate([query * k_s[j] for j in js], axis=1)
                    take = ones[: prod.shape[1], : prod.shape[1]]
                    return jnp.dot(prod, take, preferred_element_type=F32)

                if few:
                    scores = []
                    for j in range(0, n, 2):
                        js = range(j, min(j + 2, n))
                        pair = score(*js)
                        scores += [pair[:, i * width : (i + 1) * width] for i in range(len(js))]
                    top = functools.reduce(jnp.maximum, scores)
                    den, acc = None, None
                    for j in range(n):
                        e = jnp.exp2((scores[j] - top) * factor)
                        term = e * v_s[j]
                        den = e if den is None else den + e
                        acc = term if acc is None else acc + term
                else:
                    def more(j, carry):
                        top, den, acc = carry
                        sc = score(j)
                        now = jnp.maximum(top, sc)
                        keep = jnp.exp2((top - now) * factor)
                        e = jnp.exp2((sc - now) * factor)
                        return now, den * keep + e, acc * keep + e * v_s[j]

                    _, den, acc = lax.fori_loop(
                        1, n, more, (score(0), jnp.ones((cols, width), F32), v_s[0])
                    )
                mixed = (acc / den).astype(BF16)
                proj = jnp.dot(mixed, out_weight[...], preferred_element_type=F32)
                back[s, m, r] = (recv[s, m, r].astype(F32) + proj).astype(BF16)

                @pl.when(k < n - 1)
                def _():
                    to_member(s, m, r).start()

            if few:
                project(0, n)
                for k in range(n):
                    attend(k)
            else:
                pl.loop(0, n)(lambda m: project(m, 1))
                pl.loop(0, n)(attend)

        out[0, pl.ds(me * share + s * sub, sub)] = back[s, me]

    for low, high in ((0, half), (half, n)):
        @pl.loop(0, steps)
        def _(s, low=low, high=high):
            pl.loop(low, high)(lambda k: block(s, k))

    pl.loop(0, steps)(mix)

    for a, b in SIDES:
        @pl.when(exists(a, b))
        def _(a=a, b=b):
            halo_copy(a, b).wait_send()

    @pl.loop(0, steps)
    def _(s):
        @pl.loop(0, n - 1)
        def _(k):
            d = other(k)

            @pl.loop(0, sub)
            def _(r):
                to_mixer(s, d, r).wait_send()
                to_member(s, d, r).wait_send()
                from_mixer(s, d, r).wait_recv()


SUB = 4


def shards(n, row_n, col_n, *args):
    fields = args[0]
    _, rows, cols, width = fields.shape
    share = rows // n
    sub = math.gcd(share, SUB)
    steps = share // sub
    vmem = pl.BlockSpec(memory_space=pltpu.VMEM)
    dma = pltpu.SemaphoreType.DMA
    blocks = (steps, n, sub, cols, width)
    return pl.pallas_call(
        functools.partial(kernel, n, row_n, col_n, sub),
        out_shape=jax.ShapeDtypeStruct(fields.shape, fields.dtype),
        in_specs=[pl.BlockSpec(memory_space=pl.ANY)] * len(args),
        out_specs=vmem,
        scratch_shapes=[pltpu.VMEM(x.shape, x.dtype) for x in args[1:]] + [
            pltpu.VMEM(fields.shape, fields.dtype),
            dma((len(args),)),
            pltpu.VMEM((rows + 2 * HALO, cols + 2 * PAD, width), F32),
            pltpu.VMEM((KERNEL, 8, width), F32),
            pltpu.VMEM((sub, cols, width), F32),
            pltpu.VMEM(blocks, BF16),
            pltpu.VMEM(blocks, BF16),
            pltpu.VMEM(blocks, BF16),
            pltpu.VMEM((n, cols, width), BF16),
            pltpu.VMEM((n, cols, width), BF16),
            pltpu.VMEM((n, cols, width), F32),
            pltpu.VMEM((width, 3 * width), BF16),
            pltpu.VMEM((2, HALO, cols, width), BF16),
            pltpu.VMEM((2, rows, PAD, width), BF16),
            pltpu.VMEM((4, HALO, PAD, width), BF16),
            dma((8,)),
            dma((8,)),
            dma((steps, n, sub)),
            dma((steps, n, sub)),
            dma((steps, n, sub)),
            dma((steps, n, sub)),
        ],
        compiler_params=pltpu.CompilerParams(
            collective_id=0, has_side_effects=True, vmem_limit_bytes=56 * 1024 * 1024
        ),
    )(*args)


def solution(mesh):
    size = mesh.shape
    return jax.shard_map(
        functools.partial(shards, size["ens"], size["row"], size["col"]),
        mesh=mesh,
        in_specs=(P("ens", ("group", "row"), "col", None), P(), P(), P(), P(), P(), P(), P(), P()),
        out_specs=P("ens", ("group", "row"), "col", None),
        check_vma=False,
    )
```

```python
import functools
import math

import jax
import jax.numpy as jnp
from jax import lax
from jax.experimental import pallas as pl
from jax.experimental.pallas import tpu as pltpu
from jax.sharding import PartitionSpec as P

HEADS = 4
KERNEL = 7
HALO = KERNEL // 2
PAD = 16
MESH = pl.DeviceIdType.MESH
F32 = jnp.float32
BF16 = jnp.bfloat16
SIDES = [(a, b) for a in (-1, 0, 1) for b in (-1, 0, 1) if (a, b) != (0, 0)]


def norm(values, gain):
    center = values - jnp.mean(values, axis=-1, keepdims=True)
    spread = jnp.mean(center * center, axis=-1, keepdims=True)
    return (center * lax.rsqrt(spread + 1e-06) * gain).astype(BF16)


def gelu(h):
    inner = h * (0.7978845608028654 + 0.035677408136300125 * (h * h))
    return (0.5 * h) * (1.0 + jnp.tanh(inner))


def kernel(
    n, row_n, col_n, sub,
    fields_hbm, *refs,
):
    count = 8
    weights_hbm, out, weights = refs[:count], refs[count], refs[count + 1 : 2 * count + 1]
    fields, load = refs[2 * count + 1 : 2 * count + 3]
    conv_weight, conv_gain, mlp_in, mlp_out, layer_scale, attn_gain, qkv, out_weight = weights
    (
    pad, taps, conv, mid, recv, back, q_s, k_s, v_s, qkv_s, halo_rows, halo_cols, halo_corner,
    halo_send, halo_recv, send1, recv1, send2, recv2,
    ) = refs[2 * count + 3 :]
    _, rows, cols, width = fields.shape
    share = rows // n
    steps = share // sub
    me = lax.axis_index("ens")
    row_i = lax.axis_index("row")
    col_i = lax.axis_index("col")
    loads = [
        pltpu.make_async_copy(src, dst, load.at[i])
        for i, (src, dst) in enumerate(zip((fields_hbm, *weights_hbm), (fields, *weights)))
    ]
    for copy in loads:
        copy.start()
    barrier = pltpu.get_barrier_semaphore()

    def exists(a, b):
        ok = None
        for d, i, size in ((a, row_i, row_n), (b, col_i, col_n)):
            if d == 0:
                continue
            one = i > 0 if d < 0 else i < size - 1
            ok = one if ok is None else jnp.logical_and(ok, one)
        return ok

    half = n // 2 if n % 2 == 0 else n

    def other(k):
        if n % 2:
            return lax.rem(me + 1 + k, n)
        side = me // half
        far = jnp.where(side == 0, half + k, half - 1 - k)
        near = side * half + lax.rem(me + 1 + k, half)
        return jnp.where(k < half, far, near)

    for a, b in SIDES:
        @pl.when(exists(a, b))
        def _(a=a, b=b):
            pl.semaphore_signal(
                barrier, inc=1, device_id={"row": row_i + a, "col": col_i + b}, device_id_type=MESH
            )

    @pl.loop(0, n - 1)
    def _(k):
        pl.semaphore_signal(barrier, inc=1, device_id={"ens": other(k)}, device_id_type=MESH)

    def around(i, size):
        return jnp.where(i > 0, 1, 0) + jnp.where(i < size - 1, 1, 0) + 1

    pl.semaphore_wait(barrier, around(row_i, row_n) * around(col_i, col_n) + (n - 2))

    def halo_ref(a, b):
        if b == 0:
            return halo_rows.at[0 if a < 0 else 1]
        if a == 0:
            return halo_cols.at[0 if b < 0 else 1]
        return halo_corner.at[(0 if a < 0 else 2) + (0 if b < 0 else 1)]

    def halo_copy(a, b):
        r = slice(0, rows) if a == 0 else (slice(0, HALO) if a < 0 else slice(rows - HALO, rows))
        c = slice(0, cols) if b == 0 else (slice(0, PAD) if b < 0 else slice(cols - PAD, cols))
        return pltpu.make_async_remote_copy(
            src_ref=fields_hbm.at[0, r, c, :],
            dst_ref=halo_ref(-a, -b),
            send_sem=halo_send.at[SIDES.index((a, b))],
            recv_sem=halo_recv.at[SIDES.index((-a, -b))],
            device_id={"row": row_i + a, "col": col_i + b},
            device_id_type=MESH,
        )

    for a, b in SIDES:
        @pl.when(exists(a, b))
        def _(a=a, b=b):
            halo_copy(a, b).start()

    for copy in loads:
        copy.wait()
    for j in range(3):
        qkv_s[:, j * width : (j + 1) * width] = qkv[j]
    for a in range(KERNEL):
        taps[a, 0:KERNEL, :] = conv_weight[a].astype(F32)

    @pl.loop(0, rows)
    def _(r):
        pad[HALO + r, PAD : PAD + cols, :] = fields[0, r].astype(F32)

    def spot(a, b):
        r = slice(HALO, HALO + rows) if a == 0 else (
            slice(0, HALO) if a < 0 else slice(HALO + rows, 2 * HALO + rows))
        c = slice(PAD, PAD + cols) if b == 0 else (
            slice(0, PAD) if b < 0 else slice(PAD + cols, 2 * PAD + cols))
        return r, c

    def take(sides):
        for a, b in sides:
            here = exists(a, b)
            r, c = spot(a, b)

            @pl.when(here)
            def _(a=a, b=b, r=r, c=c):
                pltpu.make_async_remote_copy(
                    src_ref=halo_ref(a, b),
                    dst_ref=halo_ref(a, b),
                    send_sem=halo_send.at[SIDES.index((a, b))],
                    recv_sem=halo_recv.at[SIDES.index((a, b))],
                    device_id={"row": row_i + a, "col": col_i + b},
                    device_id_type=MESH,
                ).wait_recv()
                pad[r, c, :] = halo_ref(a, b)[...].astype(F32)

            @pl.when(jnp.logical_not(here))
            def _(r=r, c=c):
                pad[r, c, :] = jnp.zeros((r.stop - r.start, c.stop - c.start, width), F32)

    late = sub >= HALO
    take([side for side in SIDES if side[0] == 0 or not late])

    gain1 = conv_gain[...].astype(F32).reshape(1, width)
    gain2 = attn_gain[...].astype(F32).reshape(1, width)
    scale = layer_scale[...].astype(F32).reshape(1, width)
    head = width // HEADS
    ones = (
        lax.broadcasted_iota(jnp.int32, (2 * width, 2 * width), 0) // head
        == lax.broadcasted_iota(jnp.int32, (2 * width, 2 * width), 1) // head
    ).astype(F32).astype(BF16)
    factor = head**-0.5 * math.log2(math.e)

    def to_mixer(s, d, r):
        return pltpu.make_async_remote_copy(
            src_ref=mid.at[s, d, r],
            dst_ref=recv.at[s, me, r],
            send_sem=send1.at[s, d, r],
            recv_sem=recv1.at[s, me, r],
            device_id={"ens": d},
            device_id_type=MESH,
        )

    def from_member(s, d, r):
        return pltpu.make_async_remote_copy(
            src_ref=mid.at[s, d, r],
            dst_ref=recv.at[s, d, r],
            send_sem=send1.at[s, d, r],
            recv_sem=recv1.at[s, d, r],
            device_id={"ens": d},
            device_id_type=MESH,
        )

    def to_member(s, d, r):
        return pltpu.make_async_remote_copy(
            src_ref=back.at[s, d, r],
            dst_ref=out.at[0, me * share + s * sub + r],
            send_sem=send2.at[s, d, r],
            recv_sem=recv2.at[s, me, r],
            device_id={"ens": d},
            device_id_type=MESH,
        )

    def from_mixer(s, d, r):
        return pltpu.make_async_remote_copy(
            src_ref=back.at[s, d, r],
            dst_ref=out.at[0, d * share + s * sub + r],
            send_sem=send2.at[s, d, r],
            recv_sem=recv2.at[s, d, r],
            device_id={"ens": d},
            device_id_type=MESH,
        )

    def block(s, k):
        d = other(k)
        first = d * share + s * sub
        if late:
            for a, edge in ((-1, 0), (1, rows - sub)):
                pl.when(first == edge)(lambda a=a: take([side for side in SIDES if side[0] == a]))

        @pl.loop(0, cols // 16)
        def _(j):
            c0 = j * 16
            acc = [jnp.zeros((16, width), F32) for _ in range(sub)]
            for b in range(KERNEL):
                lines = [
                    pad[first + r, pl.ds(c0 + (PAD - HALO + b), 16), :]
                    for r in range(sub + KERNEL - 1)
                ]
                for a in range(KERNEL):
                    w = taps[a, b : b + 1, :]
                    acc = [acc[r] + lines[r + a] * w for r in range(sub)]
            for r in range(sub):
                conv[r, pl.ds(pl.multiple_of(c0, 16), 16), :] = acc[r]

        normed = norm(conv[...].reshape(sub * cols, width), gain1)
        branch = jnp.zeros((sub * cols, width), F32)
        units = mlp_in.shape[1]
        for u in range(0, units, units // 2):
            part = slice(u, u + units // 2)
            h = jnp.dot(normed, mlp_in[:, part], preferred_element_type=F32)
            inner = gelu(h).astype(BF16)
            branch = branch + jnp.dot(inner, mlp_out[part, :], preferred_element_type=F32)
        branch = (scale * branch).reshape(sub, cols, width)
        for r in range(sub):
            mid[s, d, r] = (fields[0, first + r].astype(F32) + branch[r]).astype(BF16)

            @pl.when(k < n - 1)
            def _(r=r):
                to_mixer(s, d, r).start()

        @pl.when(k == n - 1)
        def _():
            recv[s, me] = mid[s, me]

    few = n <= 8

    def mix(s):
        @pl.loop(0, sub)
        def _(r):
            @pl.loop(0, n - 1)
            def _(k):
                from_member(s, other(k), r).wait_recv()

            def project(m, many):
                x = recv[s, pl.ds(m, many), r].astype(F32).reshape(many * cols, width)
                normed = norm(x, gain2)
                got = jnp.dot(normed, qkv_s[...], preferred_element_type=F32)
                got = got.reshape(many, cols, 3 * width)
                q_s[pl.ds(m, many)] = got[:, :, 0:width].astype(BF16)
                k_s[pl.ds(m, many)] = got[:, :, width : 2 * width].astype(BF16)
                v_s[pl.ds(m, many)] = got[:, :, 2 * width :].astype(BF16).astype(F32)

            def attend(k):
                m = other(k)
                query = q_s[m]

                def score(*js):
                    prod = jnp.concatenate([query * k_s[j] for j in js], axis=1)
                    take = ones[: prod.shape[1], : prod.shape[1]]
                    return jnp.dot(prod, take, preferred_element_type=F32)

                if few:
                    scores = []
                    for j in range(0, n, 2):
                        js = range(j, min(j + 2, n))
                        pair = score(*js)
                        scores += [pair[:, i * width : (i + 1) * width] for i in range(len(js))]
                    top = functools.reduce(jnp.maximum, scores)
                    den, acc = None, None
                    for j in range(n):
                        e = jnp.exp2((scores[j] - top) * factor)
                        term = e * v_s[j]
                        den = e if den is None else den + e
                        acc = term if acc is None else acc + term
                else:
                    def more(j, carry):
                        top, den, acc = carry
                        sc = score(j)
                        now = jnp.maximum(top, sc)
                        keep = jnp.exp2((top - now) * factor)
                        e = jnp.exp2((sc - now) * factor)
                        return now, den * keep + e, acc * keep + e * v_s[j]

                    _, den, acc = lax.fori_loop(
                        1, n, more, (score(0), jnp.ones((cols, width), F32), v_s[0])
                    )
                mixed = (acc / den).astype(BF16)
                proj = jnp.dot(mixed, out_weight[...], preferred_element_type=F32)
                back[s, m, r] = (recv[s, m, r].astype(F32) + proj).astype(BF16)

                @pl.when(k < n - 1)
                def _():
                    to_member(s, m, r).start()

            if few:
                project(0, n)
                for k in range(n):
                    attend(k)
            else:
                pl.loop(0, n)(lambda m: project(m, 1))
                pl.loop(0, n)(attend)

        out[0, pl.ds(me * share + s * sub, sub)] = back[s, me]

    for low, high in ((0, half), (half, n)):
        @pl.loop(0, steps)
        def _(s, low=low, high=high):
            pl.loop(low, high)(lambda k: block(s, k))

    pl.loop(0, steps)(mix)

    for a, b in SIDES:
        @pl.when(exists(a, b))
        def _(a=a, b=b):
            halo_copy(a, b).wait_send()

    @pl.loop(0, steps)
    def _(s):
        @pl.loop(0, n - 1)
        def _(k):
            d = other(k)

            @pl.loop(0, sub)
            def _(r):
                to_mixer(s, d, r).wait_send()
                to_member(s, d, r).wait_send()
                from_mixer(s, d, r).wait_recv()


SUB = 4


def shards(n, row_n, col_n, *args):
    fields = args[0]
    _, rows, cols, width = fields.shape
    share = rows // n
    sub = math.gcd(share, SUB)
    steps = share // sub
    vmem = pl.BlockSpec(memory_space=pltpu.VMEM)
    dma = pltpu.SemaphoreType.DMA
    blocks = (steps, n, sub, cols, width)
    return pl.pallas_call(
        functools.partial(kernel, n, row_n, col_n, sub),
        out_shape=jax.ShapeDtypeStruct(fields.shape, fields.dtype),
        in_specs=[pl.BlockSpec(memory_space=pltpu.HBM)] * len(args),
        out_specs=vmem,
        scratch_shapes=[pltpu.VMEM(x.shape, x.dtype) for x in args[1:]] + [
            pltpu.VMEM(fields.shape, fields.dtype),
            dma((len(args),)),
            pltpu.VMEM((rows + 2 * HALO, cols + 2 * PAD, width), F32),
            pltpu.VMEM((KERNEL, 8, width), F32),
            pltpu.VMEM((sub, cols, width), F32),
            pltpu.VMEM(blocks, BF16),
            pltpu.VMEM(blocks, BF16),
            pltpu.VMEM(blocks, BF16),
            pltpu.VMEM((n, cols, width), BF16),
            pltpu.VMEM((n, cols, width), BF16),
            pltpu.VMEM((n, cols, width), F32),
            pltpu.VMEM((width, 3 * width), BF16),
            pltpu.VMEM((2, HALO, cols, width), BF16),
            pltpu.VMEM((2, rows, PAD, width), BF16),
            pltpu.VMEM((4, HALO, PAD, width), BF16),
            dma((8,)),
            dma((8,)),
            dma((steps, n, sub)),
            dma((steps, n, sub)),
            dma((steps, n, sub)),
            dma((steps, n, sub)),
        ],
        compiler_params=pltpu.CompilerParams(
            collective_id=0, has_side_effects=True, vmem_limit_bytes=56 * 1024 * 1024
        ),
    )(*args)


def solution(mesh):
    size = mesh.shape
    return jax.shard_map(
        functools.partial(shards, size["ens"], size["row"], size["col"]),
        mesh=mesh,
        in_specs=(P("ens", ("group", "row"), "col", None), P(), P(), P(), P(), P(), P(), P(), P()),
        out_specs=P("ens", ("group", "row"), "col", None),
        check_vma=False,
    )
```

```python
import functools
import math

import jax
import jax.numpy as jnp
from jax import lax
from jax.experimental import pallas as pl
from jax.experimental.pallas import tpu as pltpu
from jax.sharding import PartitionSpec as P

HEADS = 4
KERNEL = 7
HALO = KERNEL // 2
PAD = 16
PIECES = 2
MESH = pl.DeviceIdType.MESH
F32 = jnp.float32
BF16 = jnp.bfloat16
SIDES = [(a, b) for a in (-1, 0, 1) for b in (-1, 0, 1) if (a, b) != (0, 0)]


def norm(values, gain):
    center = values - jnp.mean(values, axis=-1, keepdims=True)
    spread = jnp.mean(center * center, axis=-1, keepdims=True)
    return (center * lax.rsqrt(spread + 1e-06) * gain).astype(BF16)


def gelu(h):
    inner = h * (0.7978845608028654 + 0.035677408136300125 * (h * h))
    return (0.5 * h) * (1.0 + jnp.tanh(inner))


def kernel(
    n, row_n, col_n, sub,
    fields_hbm, *refs,
):
    count = 8
    weights_hbm, out, weights = refs[:count], refs[count], refs[count + 1 : 2 * count + 1]
    fields, load = refs[2 * count + 1 : 2 * count + 3]
    conv_weight, conv_gain, mlp_in, mlp_out, layer_scale, attn_gain, qkv, out_weight = weights
    (
    pad, taps, conv, mid, recv, back, q_s, k_s, v_s, qkv_s, halo_rows, halo_cols, halo_corner,
    halo_send, halo_recv, send1, recv1, send2, recv2,
    ) = refs[2 * count + 3 :]
    _, rows, cols, width = fields.shape
    share = rows // n
    steps = share // sub
    piece = cols // PIECES
    me = lax.axis_index("ens")
    row_i = lax.axis_index("row")
    col_i = lax.axis_index("col")
    loads = [
        pltpu.make_async_copy(src, dst, load.at[i])
        for i, (src, dst) in enumerate(zip((fields_hbm, *weights_hbm), (fields, *weights)))
    ]
    for copy in loads:
        copy.start()
    barrier = pltpu.get_barrier_semaphore()

    def exists(a, b):
        ok = None
        for d, i, size in ((a, row_i, row_n), (b, col_i, col_n)):
            if d == 0:
                continue
            one = i > 0 if d < 0 else i < size - 1
            ok = one if ok is None else jnp.logical_and(ok, one)
        return ok

    half = n // 2 if n % 2 == 0 else n

    def other(k):
        if n % 2:
            return lax.rem(me + 1 + k, n)
        side = me // half
        far = jnp.where(side == 0, half + k, half - 1 - k)
        near = side * half + lax.rem(me + 1 + k, half)
        return jnp.where(k < half, far, near)

    for a, b in SIDES:
        @pl.when(exists(a, b))
        def _(a=a, b=b):
            pl.semaphore_signal(
                barrier, inc=1, device_id={"row": row_i + a, "col": col_i + b}, device_id_type=MESH
            )

    @pl.loop(0, n - 1)
    def _(k):
        pl.semaphore_signal(barrier, inc=1, device_id={"ens": other(k)}, device_id_type=MESH)

    def around(i, size):
        return jnp.where(i > 0, 1, 0) + jnp.where(i < size - 1, 1, 0) + 1

    pl.semaphore_wait(barrier, around(row_i, row_n) * around(col_i, col_n) + (n - 2))

    def halo_ref(a, b):
        if b == 0:
            return halo_rows.at[0 if a < 0 else 1]
        if a == 0:
            return halo_cols.at[0 if b < 0 else 1]
        return halo_corner.at[(0 if a < 0 else 2) + (0 if b < 0 else 1)]

    def halo_copy(a, b):
        r = slice(0, rows) if a == 0 else (slice(0, HALO) if a < 0 else slice(rows - HALO, rows))
        c = slice(0, cols) if b == 0 else (slice(0, PAD) if b < 0 else slice(cols - PAD, cols))
        return pltpu.make_async_remote_copy(
            src_ref=fields_hbm.at[0, r, c, :],
            dst_ref=halo_ref(-a, -b),
            send_sem=halo_send.at[SIDES.index((a, b))],
            recv_sem=halo_recv.at[SIDES.index((-a, -b))],
            device_id={"row": row_i + a, "col": col_i + b},
            device_id_type=MESH,
        )

    for a, b in SIDES:
        @pl.when(exists(a, b))
        def _(a=a, b=b):
            halo_copy(a, b).start()

    for copy in loads:
        copy.wait()
    for j in range(3):
        qkv_s[:, j * width : (j + 1) * width] = qkv[j]
    for a in range(KERNEL):
        taps[a, 0:KERNEL, :] = conv_weight[a].astype(F32)

    @pl.loop(0, rows)
    def _(r):
        pad[HALO + r, PAD : PAD + cols, :] = fields[0, r].astype(F32)

    def spot(a, b):
        r = slice(HALO, HALO + rows) if a == 0 else (
            slice(0, HALO) if a < 0 else slice(HALO + rows, 2 * HALO + rows))
        c = slice(PAD, PAD + cols) if b == 0 else (
            slice(0, PAD) if b < 0 else slice(PAD + cols, 2 * PAD + cols))
        return r, c

    def take(sides):
        for a, b in sides:
            here = exists(a, b)
            r, c = spot(a, b)

            @pl.when(here)
            def _(a=a, b=b, r=r, c=c):
                pltpu.make_async_remote_copy(
                    src_ref=halo_ref(a, b),
                    dst_ref=halo_ref(a, b),
                    send_sem=halo_send.at[SIDES.index((a, b))],
                    recv_sem=halo_recv.at[SIDES.index((a, b))],
                    device_id={"row": row_i + a, "col": col_i + b},
                    device_id_type=MESH,
                ).wait_recv()
                pad[r, c, :] = halo_ref(a, b)[...].astype(F32)

            @pl.when(jnp.logical_not(here))
            def _(r=r, c=c):
                pad[r, c, :] = jnp.zeros((r.stop - r.start, c.stop - c.start, width), F32)

    late = sub >= HALO
    take([side for side in SIDES if side[0] == 0 or not late])

    gain1 = conv_gain[...].astype(F32).reshape(1, width)
    gain2 = attn_gain[...].astype(F32).reshape(1, width)
    scale = layer_scale[...].astype(F32).reshape(1, width)
    head = width // HEADS
    ones = (
        lax.broadcasted_iota(jnp.int32, (2 * width, 2 * width), 0) // head
        == lax.broadcasted_iota(jnp.int32, (2 * width, 2 * width), 1) // head
    ).astype(F32).astype(BF16)
    factor = head**-0.5 * math.log2(math.e)

    def to_mixer(s, d, r):
        return pltpu.make_async_remote_copy(
            src_ref=mid.at[s, d, r],
            dst_ref=recv.at[s, me, r],
            send_sem=send1.at[s, d, r],
            recv_sem=recv1.at[s, me, r],
            device_id={"ens": d},
            device_id_type=MESH,
        )

    def from_member(s, d, r):
        return pltpu.make_async_remote_copy(
            src_ref=mid.at[s, d, r],
            dst_ref=recv.at[s, d, r],
            send_sem=send1.at[s, d, r],
            recv_sem=recv1.at[s, d, r],
            device_id={"ens": d},
            device_id_type=MESH,
        )

    def to_member(s, d, r):
        return pltpu.make_async_remote_copy(
            src_ref=back.at[s, d, r],
            dst_ref=out.at[0, pl.ds(me * share + s * sub, sub), pl.ds(pl.multiple_of(r * piece, 16), piece)],
            send_sem=send2.at[s, d, r],
            recv_sem=recv2.at[s, me, r],
            device_id={"ens": d},
            device_id_type=MESH,
        )

    def from_mixer(s, d, r):
        return pltpu.make_async_remote_copy(
            src_ref=back.at[s, d, r],
            dst_ref=out.at[0, pl.ds(d * share + s * sub, sub), pl.ds(pl.multiple_of(r * piece, 16), piece)],
            send_sem=send2.at[s, d, r],
            recv_sem=recv2.at[s, d, r],
            device_id={"ens": d},
            device_id_type=MESH,
        )

    def block(s, k):
        d = other(k)
        first = d * share + s * sub
        if late:
            for a, edge in ((-1, 0), (1, rows - sub)):
                pl.when(first == edge)(lambda a=a: take([side for side in SIDES if side[0] == a]))

        @pl.loop(0, PIECES)
        def _(p):
            start = pl.multiple_of(p * piece, 16)

            @pl.loop(0, piece // 16)
            def _(j):
                c0 = start + j * 16
                acc = [jnp.zeros((16, width), F32) for _ in range(sub)]
                for b in range(KERNEL):
                    lines = [
                        pad[first + r, pl.ds(c0 + (PAD - HALO + b), 16), :]
                        for r in range(sub + KERNEL - 1)
                    ]
                    for a in range(KERNEL):
                        w = taps[a, b : b + 1, :]
                        acc = [acc[r] + lines[r + a] * w for r in range(sub)]
                for r in range(sub):
                    conv[r, pl.ds(pl.multiple_of(j * 16, 16), 16), :] = acc[r]

            normed = norm(conv[...].reshape(sub * piece, width), gain1)
            branch = jnp.zeros((sub * piece, width), F32)
            units = mlp_in.shape[1]
            for u in range(0, units, units // 2):
                part = slice(u, u + units // 2)
                h = jnp.dot(normed, mlp_in[:, part], preferred_element_type=F32)
                inner = gelu(h).astype(BF16)
                branch = branch + jnp.dot(inner, mlp_out[part, :], preferred_element_type=F32)
            branch = (scale * branch).reshape(sub, piece, width)
            kept = fields[0, pl.ds(first, sub), pl.ds(start, piece), :].astype(F32)
            mid[s, d, p] = (kept + branch).astype(BF16)

            @pl.when(k < n - 1)
            def _():
                to_mixer(s, d, p).start()

        @pl.when(k == n - 1)
        def _():
            recv[s, me] = mid[s, me]

    few = n <= 8

    def mix(s):
        @pl.loop(0, PIECES)
        def _(r):
            @pl.loop(0, n - 1)
            def _(k):
                from_member(s, other(k), r).wait_recv()

            def project(m, many):
                x = recv[s, pl.ds(m, many), r].astype(F32).reshape(many * sub * piece, width)
                normed = norm(x, gain2)
                got = jnp.dot(normed, qkv_s[...], preferred_element_type=F32)
                got = got.reshape(many, sub * piece, 3 * width)
                q_s[pl.ds(m, many)] = got[:, :, 0:width].astype(BF16)
                k_s[pl.ds(m, many)] = got[:, :, width : 2 * width].astype(BF16)
                v_s[pl.ds(m, many)] = got[:, :, 2 * width :].astype(BF16).astype(F32)

            def attend(k):
                m = other(k)
                query = q_s[m]

                def score(*js):
                    prod = jnp.concatenate([query * k_s[j] for j in js], axis=1)
                    take = ones[: prod.shape[1], : prod.shape[1]]
                    return jnp.dot(prod, take, preferred_element_type=F32)

                if few:
                    scores = []
                    for j in range(0, n, 2):
                        js = range(j, min(j + 2, n))
                        pair = score(*js)
                        scores += [pair[:, i * width : (i + 1) * width] for i in range(len(js))]
                    top = functools.reduce(jnp.maximum, scores)
                    den, acc = None, None
                    for j in range(n):
                        e = jnp.exp2((scores[j] - top) * factor)
                        term = e * v_s[j]
                        den = e if den is None else den + e
                        acc = term if acc is None else acc + term
                else:
                    def more(j, carry):
                        top, den, acc = carry
                        sc = score(j)
                        now = jnp.maximum(top, sc)
                        keep = jnp.exp2((top - now) * factor)
                        e = jnp.exp2((sc - now) * factor)
                        return now, den * keep + e, acc * keep + e * v_s[j]

                    _, den, acc = lax.fori_loop(
                        1, n, more, (score(0), jnp.ones((sub * piece, width), F32), v_s[0])
                    )
                mixed = (acc / den).astype(BF16)
                proj = jnp.dot(mixed, out_weight[...], preferred_element_type=F32)
                back[s, m, r] = (recv[s, m, r].astype(F32) + proj.reshape(sub, piece, width)).astype(BF16)

                @pl.when(k < n - 1)
                def _():
                    to_member(s, m, r).start()

            if few:
                project(0, n)
                for k in range(n):
                    attend(k)
            else:
                pl.loop(0, n)(lambda m: project(m, 1))
                pl.loop(0, n)(attend)

        for p in range(PIECES):
            rows_here = pl.ds(me * share + s * sub, sub)
            out[0, rows_here, p * piece : (p + 1) * piece, :] = back[s, me, p]

    for low, high in ((0, half), (half, n)):
        @pl.loop(0, steps)
        def _(s, low=low, high=high):
            pl.loop(low, high)(lambda k: block(s, k))

    pl.loop(0, steps)(mix)

    for a, b in SIDES:
        @pl.when(exists(a, b))
        def _(a=a, b=b):
            halo_copy(a, b).wait_send()

    @pl.loop(0, steps)
    def _(s):
        @pl.loop(0, n - 1)
        def _(k):
            d = other(k)

            @pl.loop(0, PIECES)
            def _(r):
                to_mixer(s, d, r).wait_send()
                to_member(s, d, r).wait_send()
                from_mixer(s, d, r).wait_recv()


SUB = 4


def shards(n, row_n, col_n, *args):
    fields = args[0]
    _, rows, cols, width = fields.shape
    share = rows // n
    sub = math.gcd(share, SUB)
    steps = share // sub
    vmem = pl.BlockSpec(memory_space=pltpu.VMEM)
    dma = pltpu.SemaphoreType.DMA
    piece = cols // PIECES
    blocks = (steps, n, PIECES, sub, piece, width)
    return pl.pallas_call(
        functools.partial(kernel, n, row_n, col_n, sub),
        out_shape=jax.ShapeDtypeStruct(fields.shape, fields.dtype),
        in_specs=[pl.BlockSpec(memory_space=pltpu.HBM)] * len(args),
        out_specs=vmem,
        scratch_shapes=[pltpu.VMEM(x.shape, x.dtype) for x in args[1:]] + [
            pltpu.VMEM(fields.shape, fields.dtype),
            dma((len(args),)),
            pltpu.VMEM((rows + 2 * HALO, cols + 2 * PAD, width), F32),
            pltpu.VMEM((KERNEL, 8, width), F32),
            pltpu.VMEM((sub, piece, width), F32),
            pltpu.VMEM(blocks, BF16),
            pltpu.VMEM(blocks, BF16),
            pltpu.VMEM(blocks, BF16),
            pltpu.VMEM((n, sub * piece, width), BF16),
            pltpu.VMEM((n, sub * piece, width), BF16),
            pltpu.VMEM((n, sub * piece, width), F32),
            pltpu.VMEM((width, 3 * width), BF16),
            pltpu.VMEM((2, HALO, cols, width), BF16),
            pltpu.VMEM((2, rows, PAD, width), BF16),
            pltpu.VMEM((4, HALO, PAD, width), BF16),
            dma((8,)),
            dma((8,)),
            dma((steps, n, PIECES)),
            dma((steps, n, PIECES)),
            dma((steps, n, PIECES)),
            dma((steps, n, PIECES)),
        ],
        compiler_params=pltpu.CompilerParams(
            collective_id=0, has_side_effects=True, vmem_limit_bytes=56 * 1024 * 1024
        ),
    )(*args)


def solution(mesh):
    size = mesh.shape
    return jax.shard_map(
        functools.partial(shards, size["ens"], size["row"], size["col"]),
        mesh=mesh,
        in_specs=(P("ens", ("group", "row"), "col", None), P(), P(), P(), P(), P(), P(), P(), P()),
        out_specs=P("ens", ("group", "row"), "col", None),
        check_vma=False,
    )
```
